512 devices in a mesh: space: 128 (over x, y, z_lo), vz: 4 (over z_hi, core).
Axes of the slice: x: 4, y: 8, z: 8 (z_hi: 2, z_lo: 4; z = z_hi * 4 + z_lo), core: 2. Of those that a mesh axis runs over, the one named last changes fastest.
Arguments:
- distribution: float32 [48, 256, 8, 2304], P('vz', 'space'), may hold values from 0 to 6, as said below
- collision_rate: float32 [256, 8], P('space'), may hold values from 0.5 to 2
Outputs:
- new_distribution: float32 [48, 256, 8, 2304], P('vz', 'space')
The draws below stay inside these ranges and needn't reach their ends.
Inputs may be any that keep to these rules, and one draw needn't show every extreme that they name: `distribution`: every entry is positive.
All inputs are finite; a program needn't handle non-finite values.
Results may differ from the reference program's by a relative error of at most 0.000056.
Values sent between devices are 32-bit elements; how exact they have to be, the bound alone decides.
No kernel may reach another device: no remote copies, remote signals or barrier semaphores. Data moves between devices by JAX's collectives and lax.ppermute only.
A program may use at most 64 MiB of HBM per device.

```python
import math
import jax
import jax.numpy as jnp
from jax import lax

V = 48
NY = 8
SWEEPS = 3
NX = 256


def draw_distribution(key, part):
    key_list = jax.random.split(key, 6)
    grid_values = 4.5 * (2.0 * jnp.arange(V, dtype=jnp.float32) + 1.0 - V) / V
    speed_x = jnp.repeat(grid_values, V)
    speed_y = jnp.tile(grid_values, V)
    speed_z = grid_values[:, None, None, None]
    cell_shape = (1, NX, NY, 1)
    full_shape = (V, NX, NY, V * V)
    mass_density = jnp.exp(jax.random.uniform(key_list[0], cell_shape, jnp.float32, math.log(0.3), math.log(3.0)))
    roughness = jnp.exp(jax.random.uniform(key_list[1], full_shape, jnp.float32, math.log(0.5), math.log(2.0)))
    spread_t = jnp.exp(jax.random.uniform(key_list[2], cell_shape, jnp.float32, math.log(1.5), math.log(4.0)))
    drift_velocity_x = jax.random.uniform(key_list[3], cell_shape, jnp.float32, -0.8, 0.8)
    drift_velocity_y = jax.random.uniform(key_list[4], cell_shape, jnp.float32, -0.8, 0.8)
    drift_velocity_z = jax.random.uniform(key_list[5], cell_shape, jnp.float32, 0.2, 0.8)
    profile = jnp.exp(-((speed_x - drift_velocity_x) ** 2 + (speed_y - drift_velocity_y) ** 2 + (speed_z - drift_velocity_z) ** 2) / (2.0 * spread_t))
    return (mass_density * profile * roughness).astype(jnp.float32)


def levels(stream_key, shape, shards, smallest, top_value):
    gain, own = 1.0, jax.random.fold_in(stream_key, 6)
    for dim, parts in shards:
        heights = jnp.exp(jax.random.uniform(jax.random.fold_in(own, dim), (parts,), jnp.float32, smallest / len(shards), top_value / len(shards)))
        gain = gain * jnp.repeat(heights, shape[dim] // parts).reshape([-1 if axis == dim else 1 for axis in range(len(shape))])
    return gain


def setup_inputs(seed: int = 0) -> dict:
    key_of = jax.random.split(jax.random.key(seed), 3)
    return {
        "distribution": draw_distribution(jax.random.fold_in(key_of[2], 71), 0),
        "collision_rate": jnp.clip(jnp.exp(math.log(2.0) - 1.3862944 * jax.random.uniform(key_of[1], (NX, NY), jnp.float32) ** levels(key_of[1], (NX, NY), ((0, 128),), -0.2, 0.2)), 0.5, 2.0),
    }


vel_max = 4.5
step_ratio = 0.1
collision_scale = 0.004
relax_scale = 0.5


def grid_speeds(position):
    return vel_max * (2.0 * position + 1.0 - V) / V


def velocity_columns():
    grid_values = grid_speeds(jnp.arange(V, dtype=jnp.float32))
    return jnp.repeat(grid_values, V), jnp.tile(grid_values, V)


def beam_warming(middle, near_cells, far_cells, magnitude):
    return middle - 0.5 * magnitude * (3.0 * middle - 4.0 * near_cells + far_cells) + 0.5 * magnitude * magnitude * (middle - 2.0 * near_cells + far_cells)


def roll_transport(field_data, speed_cols, axis_id):
    positive = speed_cols > 0
    near_cells = jnp.where(positive, jnp.roll(field_data, 1, axis_id), jnp.roll(field_data, -1, axis_id))
    far_cells = jnp.where(positive, jnp.roll(field_data, 2, axis_id), jnp.roll(field_data, -2, axis_id))
    return beam_warming(field_data, near_cells, far_cells, step_ratio * jnp.abs(speed_cols))


def combine_planes(partial_value, vertical_speeds):
    zero_moment = partial_value[0]
    return jnp.stack([jnp.sum(zero_moment, 0), jnp.sum(partial_value[1], 0), jnp.sum(partial_value[2], 0), jnp.sum(vertical_speeds * zero_moment, 0), jnp.sum(partial_value[3] + vertical_speeds * vertical_speeds * zero_moment, 0)])


def cell_state(moment_totals):
    grid_spacing = 2.0 * vel_max / V
    unnormalised_mass = moment_totals[0]
    drift_velocity_x = moment_totals[1] / unnormalised_mass
    drift_velocity_y = moment_totals[2] / unnormalised_mass
    drift_velocity_z = moment_totals[3] / unnormalised_mass
    thermal_energy = (moment_totals[4] / unnormalised_mass - drift_velocity_x * drift_velocity_x - drift_velocity_y * drift_velocity_y - drift_velocity_z * drift_velocity_z) / 3.0
    return unnormalised_mass * grid_spacing ** 3, drift_velocity_x, drift_velocity_y, drift_velocity_z, thermal_energy


def maxwellian(cell_entries, velocity_x_grid, velocity_y_grid, vertical_speeds):
    mass_density, drift_velocity_x, drift_velocity_y, drift_velocity_z, thermal_energy = cell_entries
    squared_spread = (velocity_x_grid - drift_velocity_x) ** 2 + (velocity_y_grid - drift_velocity_y) ** 2 + (vertical_speeds - drift_velocity_z) ** 2
    return mass_density * (2.0 * jnp.pi * thermal_energy) ** -1.5 * jnp.exp(-squared_spread / (2.0 * thermal_energy))


def velocity_shifts(middle):
    zero_row = jnp.zeros(middle.shape[:-1] + (V,), middle.dtype)
    zero_one = jnp.zeros(middle.shape[:-1] + (1,), middle.dtype)
    upper_x_neighbour = jnp.concatenate([middle[..., V:], zero_row], axis=-1)
    lower_x_neighbour = jnp.concatenate([zero_row, middle[..., :-V]], axis=-1)
    upper_y_neighbour = jnp.concatenate([middle[..., 1:], zero_one], axis=-1)
    lower_y_neighbour = jnp.concatenate([zero_one, middle[..., :-1]], axis=-1)
    return upper_x_neighbour, lower_x_neighbour, upper_y_neighbour, lower_y_neighbour


def relaxation_pass(bordered_grid, forcing_term, diagonal_factor, vertical_speeds, cell_entries, collide_rate, velocity_x_grid, velocity_y_grid, upper_mask, lower_mask):
    mass_density, drift_velocity_x, drift_velocity_y, drift_velocity_z, thermal_energy = cell_entries
    grid_spacing = 2.0 * vel_max / V
    stiffness_factor = thermal_energy / (grid_spacing * grid_spacing)
    half_timestep = 0.5 / grid_spacing
    middle = bordered_grid[1:-1]
    upper_x_neighbour, lower_x_neighbour, upper_y_neighbour, lower_y_neighbour = velocity_shifts(middle)
    running_total = forcing_term + collide_rate * ((stiffness_factor + (velocity_x_grid + grid_spacing - drift_velocity_x) * half_timestep) * upper_x_neighbour + (stiffness_factor - (velocity_x_grid - grid_spacing - drift_velocity_x) * half_timestep) * lower_x_neighbour)
    running_total = running_total + collide_rate * ((stiffness_factor + (velocity_y_grid + grid_spacing - drift_velocity_y) * half_timestep) * upper_mask * upper_y_neighbour + (stiffness_factor - (velocity_y_grid - grid_spacing - drift_velocity_y) * half_timestep) * lower_mask * lower_y_neighbour)
    running_total = running_total + collide_rate * ((stiffness_factor + (vertical_speeds + grid_spacing - drift_velocity_z) * half_timestep) * bordered_grid[2:] + (stiffness_factor - (vertical_speeds - grid_spacing - drift_velocity_z) * half_timestep) * bordered_grid[:-2])
    return running_total / diagonal_factor


def reference(distribution, collision_rate):
    velocity_x_grid, velocity_y_grid = velocity_columns()
    weights = jnp.stack([jnp.ones_like(velocity_x_grid), velocity_x_grid, velocity_y_grid, velocity_x_grid * velocity_x_grid + velocity_y_grid * velocity_y_grid], axis=1)

    def transport_plane(plane):
        swept_x = roll_transport(plane, velocity_x_grid, 0)
        partial_sums = jnp.einsum("xyk,kw->wxy", plane, weights, precision=lax.Precision.HIGHEST)
        return roll_transport(swept_x, velocity_y_grid, 1), partial_sums

    transported, partial_value = lax.map(transport_plane, distribution)
    speeds_all = grid_speeds(jnp.arange(V, dtype=jnp.float32))
    moment_totals = combine_planes(jnp.moveaxis(partial_value, 1, 0), speeds_all[:, None, None])
    state_all = cell_state(moment_totals)
    index_y = jnp.arange(V * V, dtype=jnp.int32) % V
    upper_mask = (index_y < V - 1).astype(jnp.float32)
    lower_mask = (index_y > 0).astype(jnp.float32)
    vertical_speeds = speeds_all[:, None, None]
    grid_spacing = 2.0 * vel_max / V

    def column(column_id):
        field_data = lax.dynamic_index_in_dim(transported, column_id, 1, keepdims=False)
        cell_entries = tuple(lax.dynamic_index_in_dim(entry_array, column_id, 0, keepdims=False)[None, :, None] for entry_array in state_all)
        pointwise_rate = lax.dynamic_index_in_dim(collision_rate, column_id, 0, keepdims=False)[None, :, None]
        collide_rate = collision_scale * pointwise_rate
        relaxation_rate = relax_scale * pointwise_rate
        stiffness_factor = cell_entries[4] / (grid_spacing * grid_spacing)
        diagonal_factor = 1.0 + relaxation_rate + 6.0 * collide_rate * stiffness_factor
        forcing_term = field_data + relaxation_rate * maxwellian(cell_entries, velocity_x_grid, velocity_y_grid, vertical_speeds)
        current_guess = field_data
        for sweep_id in range(SWEEPS):
            bordered_grid = jnp.pad(current_guess, ((1, 1), (0, 0), (0, 0)))
            current_guess = relaxation_pass(bordered_grid, forcing_term, diagonal_factor, vertical_speeds, cell_entries, collide_rate, velocity_x_grid, velocity_y_grid, upper_mask, lower_mask)
        return current_guess

    columns = lax.map(column, jnp.arange(NX, dtype=jnp.int32))
    return jnp.moveaxis(columns, 0, 1)
```

```python
import functools
import math

import jax
import jax.numpy as jnp
from jax import lax
from jax.experimental import pallas as pl
from jax.experimental.pallas import tpu as pltpu
from jax.sharding import PartitionSpec as P

V = 48
WIDTH = V * V
HALF = WIDTH // 2
DEPTH = 3

vel_max = 4.5
step_ratio = 0.1
collision_scale = 0.004
relax_scale = 0.5
spacing = 2.0 * vel_max / V

VMEM_LIMIT = 40 * 1024 * 1024


def speed_of(position):
    return vel_max * (2.0 * position - (V - 1.0)) / V


def lane_grid(first, width, rows=8):
    lane = lax.broadcasted_iota(jnp.int32, (rows, width), 1).astype(jnp.float32) + float(first)
    column = jnp.floor((lane + 0.5) * (1.0 / V))
    return column, lane - V * column


def wide(tile):
    return jnp.concatenate([tile] * (WIDTH // 128), axis=1)


def moments_kernel(slab_ref, f_ref, out_ref):
    planes, columns = f_ref.shape[0], f_ref.shape[1]
    slab = slab_ref[0]
    chunk = 768
    lane = lax.broadcasted_iota(jnp.int32, (8, 128), 1)
    for column in range(columns):
        totals = [jnp.zeros((8, 1), jnp.float32)] * 5
        for first in range(0, WIDTH, chunk):
            mass = jnp.zeros((8, chunk), jnp.float32)
            flow = jnp.zeros((8, chunk), jnp.float32)
            heat = jnp.zeros((8, chunk), jnp.float32)
            for plane in range(planes):
                cz = speed_of((slab * planes + plane).astype(jnp.float32))
                f = f_ref[plane, column, :, first : first + chunk]
                scaled = f * cz
                mass += f
                flow += scaled
                heat += scaled * cz
            vx, vy = lane_grid(first, chunk)
            cx, cy = speed_of(vx), speed_of(vy)
            parts = (mass, mass * cx, mass * cy, flow, mass * (cx * cx + cy * cy) + heat)
            totals = [t + jnp.sum(p, axis=1, keepdims=True) for t, p in zip(totals, parts)]
        row = jnp.zeros((8, 128), jnp.float32)
        for k in range(5):
            row = jnp.where(lane == k, totals[k], row)
        out_ref[column] = row


def coefficients_kernel(total_ref, rate_ref, coef_ref, cell_ref):
    for column in range(total_ref.shape[0]):
        m0, m1, m2, m3, m4 = (
            jnp.broadcast_to(total_ref[column, :, k : k + 1], (8, 128)) for k in range(5)
        )
        rate = rate_ref[column]
        density = m0 * spacing**3
        ux, uy, uz = m1 / m0, m2 / m0, m3 / m0
        temperature = (m4 / m0 - ux * ux - uy * uy - uz * uz) / 3.0
        stiff = temperature / (spacing * spacing)
        collide, relax = collision_scale * rate, relax_scale * rate
        inverse = 1.0 / (1.0 + relax + 6.0 * collide * stiff)
        middle = collide * inverse * (stiff + 0.5)
        slope = collide * inverse * (0.5 / spacing)
        root = 1.0 / jnp.sqrt(2.0 * math.pi * temperature)
        scale = density * (root * root * root) * (relax * inverse)
        for k, value in enumerate((middle, slope, uz, temperature, inverse)):
            cell_ref[column, k] = value
        vx, vy = lane_grid(0, WIDTH)
        dx, dy = speed_of(vx) - wide(ux), speed_of(vy) - wide(uy)
        middle, slope = wide(middle), wide(slope)
        coef_ref[column, 0] = jnp.where(vx < V - 1.5, middle + slope * dx, 0.0)
        coef_ref[column, 1] = jnp.where(vx > 0.5, middle - slope * dx, 0.0)
        coef_ref[column, 2] = jnp.where(vy < V - 1.5, middle + slope * dy, 0.0)
        coef_ref[column, 3] = jnp.where(vy > 0.5, middle - slope * dy, 0.0)
        coef_ref[column, 4] = wide(scale) * jnp.exp(
            -(dx * dx + dy * dy) / (2.0 * wide(temperature))
        )


def upwind_weights(speed):
    a = step_ratio * jnp.abs(speed)
    return 1.0 - 1.5 * a + 0.5 * a * a, 2.0 * a - a * a, 0.5 * a * a - 0.5 * a


def fill_weights(weight_ref):
    vx, vy = lane_grid(0, WIDTH)
    for k, value in enumerate(upwind_weights(speed_of(vx)) + upwind_weights(speed_of(vy))):
        weight_ref[k] = value
    weight_ref[6] = jnp.where(vy > V // 2 - 0.5, 1.0, 0.0)


def transport_plane(f_ref, plane, low_ref, high_ref, entry, weight_ref, store):
    for column in range(2):
        for part in range(2):
            lanes = pl.ds(part * HALF, HALF)
            f = f_ref[plane, column, :, lanes]
            if part == 1:
                near = low_ref[entry, 1] if column == 0 else f_ref[plane, 0, :, lanes]
                far = low_ref[entry, column]
            else:
                near = f_ref[plane, 1, :, lanes] if column == 0 else high_ref[entry, 0]
                far = high_ref[entry, column]
            swept = (
                weight_ref[0, :, lanes] * f
                + weight_ref[1, :, lanes] * near
                + weight_ref[2, :, lanes] * far
            )
            positive = weight_ref[6, :, lanes] > 0.5
            near = jnp.where(positive, pltpu.roll(swept, 1, 0), pltpu.roll(swept, 7, 0))
            far = jnp.where(positive, pltpu.roll(swept, 2, 0), pltpu.roll(swept, 6, 0))
            store(
                column,
                lanes,
                weight_ref[3, :, lanes] * swept
                + weight_ref[4, :, lanes] * near
                + weight_ref[5, :, lanes] * far,
            )


def edges_kernel(slab_ref, f_ref, low_ref, high_ref, outer_ref, inner_ref, weight_ref):
    planes = f_ref.shape[0]
    odd = lax.rem(slab_ref[0], 2)
    fill_weights(weight_ref)
    for side, target in ((0, outer_ref), (1, inner_ref)):

        def step(k, carry, side=side, target=target):
            place = k + side * DEPTH
            entry = jnp.where(odd == 1, 2 * DEPTH - 1 - place, place)
            plane = jnp.where(entry < DEPTH, entry, entry + planes - 2 * DEPTH)

            def store(column, lanes, value):
                target[k, column, :, lanes] = value

            transport_plane(f_ref, plane, low_ref, high_ref, entry, weight_ref, store)
            return carry

        lax.fori_loop(0, DEPTH, step, 0)


def plane_speed(slab, odd, planes, place):
    position = slab * planes + jnp.where(odd == 1, planes - 1 - place, place)
    return speed_of(position.astype(jnp.float32))


def source_row(guess, coef_ref, cell_ref, column, cz):
    distance = cz - cell_ref[column, 2]
    fall = jnp.exp(-(distance * distance) / (2.0 * cell_ref[column, 3]))
    return wide(cell_ref[column, 4]) * guess + wide(fall) * coef_ref[column, 4]


def sweep_row(source, guess, after, before, coef_ref, cell_ref, column, cz, sign):
    tilt = sign * cell_ref[column, 1] * (cz - cell_ref[column, 2])
    middle = cell_ref[column, 0]
    total = source + wide(middle + tilt) * after + wide(middle - tilt) * before
    total += coef_ref[column, 0] * pltpu.roll(guess, WIDTH - V, 1)
    total += coef_ref[column, 1] * pltpu.roll(guess, V, 1)
    total += coef_ref[column, 2] * pltpu.roll(guess, WIDTH - 1, 1)
    total += coef_ref[column, 3] * pltpu.roll(guess, 1, 1)
    return total


def main_kernel(
    slab_ref, f_ref, low_ref, high_ref, outer_ref, inner_ref, halo_ref, coef_ref, cell_ref,
    out_ref, kept_ref, weight_ref, zero_ref, source_ref, one_ref, two_ref,
):
    planes = f_ref.shape[0]
    slab = slab_ref[0]
    odd = lax.rem(slab, 2)
    sign = jnp.where(odd == 1, -1.0, 1.0)
    fill_weights(weight_ref)
    for k in range(DEPTH):
        zero_ref[k] = outer_ref[k]
        zero_ref[planes - DEPTH + k] = inner_ref[k]
        zero_ref[planes + k] = halo_ref[DEPTH - 1 - k]

    def transport_step(k, carry):
        place = DEPTH + k
        plane = jnp.where(odd == 1, planes - 1 - place, place)

        def store(column, lanes, value):
            zero_ref[place, column, :, lanes] = value

        transport_plane(f_ref, plane, low_ref, high_ref, plane - DEPTH, weight_ref, store)
        return carry

    lax.fori_loop(0, planes - 2 * DEPTH, transport_step, 0)

    def source_step(place, carry):
        cz = plane_speed(slab, odd, planes, place)
        for column in range(2):
            source_ref[place, column] = source_row(
                zero_ref[place, column], coef_ref, cell_ref, column, cz
            )
        return carry

    lax.fori_loop(0, planes + DEPTH - 1, source_step, 0)

    def sweep(old, new, first, last, flip=False):
        def step(place, carry):
            cz = plane_speed(slab, odd, planes, place)
            spot = jnp.where(odd == 1, planes - 1 - place, place) if flip else place
            for column in range(2):
                new[spot, column] = sweep_row(
                    source_ref[place, column], old[place, column], old[place + 1, column],
                    old[place - 1, column], coef_ref, cell_ref, column, cz, sign,
                )
            return carry

        lax.fori_loop(first, last, step, 0)

    sweep(zero_ref, one_ref, 1, planes + 2)
    sweep(one_ref, two_ref, 2, planes + 1)
    sweep(two_ref, out_ref, 3, planes, flip=True)
    for k, (ref, place) in enumerate(
        ((source_ref, 0), (source_ref, 1), (source_ref, 2), (one_ref, 1), (one_ref, 2), (two_ref, 2), (two_ref, 3))
    ):
        kept_ref[k] = ref[place]


def last_kernel(
    slab_ref, halo_ref, outer_ref, kept_ref, coef_ref, cell_ref, before_ref, out_ref,
    zero_ref, source_ref, one_ref, two_ref,
):
    planes = slab_ref[1]
    slab = slab_ref[0]
    odd = lax.rem(slab, 2)
    sign = jnp.where(odd == 1, -1.0, 1.0)
    inside = jnp.where((slab == 0) | (slab == slab_ref[2] - 1), 0.0, 1.0)
    for k in range(DEPTH):
        zero_ref[k] = halo_ref[DEPTH - 1 - k]
        source_ref[DEPTH + k] = kept_ref[k]
    for k in range(2):
        zero_ref[DEPTH + k] = outer_ref[k]
        one_ref[DEPTH + 1 + k] = kept_ref[3 + k]
        two_ref[DEPTH + 2 + k] = kept_ref[5 + k]

    for place in (-2, -1):
        cz = plane_speed(slab, odd, planes, place)
        for column in range(2):
            source_ref[place + 3, column] = source_row(
                zero_ref[place + 3, column], coef_ref, cell_ref, column, cz
            )

    def sweep(old, new, first, flip=False):
        def step(k, carry):
            place = first + k
            cz = plane_speed(slab, odd, planes, place)
            gain = jnp.where(place < 0, inside, 1.0)
            spot = jnp.where(odd == 1, DEPTH - 1 - place, place) if flip else place + 3
            for column in range(2):
                new[spot, column] = gain * sweep_row(
                    source_ref[place + 3, column], old[place + 3, column], old[place + 4, column],
                    old[place + 2, column], coef_ref, cell_ref, column, cz, sign,
                )
            return carry

        lax.fori_loop(0, DEPTH, step, 0)

    sweep(zero_ref, one_ref, -2)
    sweep(one_ref, two_ref, -1)
    sweep(two_ref, out_ref, 0, flip=True)


def shape(*dims):
    return jax.ShapeDtypeStruct(dims, jnp.float32)


PARAMS = pltpu.CompilerParams(vmem_limit_bytes=VMEM_LIMIT)
SMEM = pl.BlockSpec(memory_space=pltpu.SMEM)
VMEM = pl.BlockSpec(memory_space=pltpu.VMEM)


def shards(distribution, collision_rate):
    planes, columns, rows, width = distribution.shape
    spaces, slabs = lax.axis_size("space"), lax.axis_size("vz")
    slab = lax.axis_index("vz").astype(jnp.int32)
    facts = jnp.stack([slab, jnp.int32(planes), jnp.int32(slabs)])

    forward = [(i, (i + 1) % spaces) for i in range(spaces)]
    backward = [(b, a) for a, b in forward]
    partners = [(i, i ^ 1) for i in range(slabs)]
    crossing = [(i, i + 1) for i in range(1, slabs - 1, 2)]
    crossing += [(b, a) for a, b in crossing]
    opposite = [(i, slabs - 1 - i) for i in range(slabs)]

    def both_ways(block):
        return (
            lax.ppermute(block[..., HALF:], "space", forward),
            lax.ppermute(block[..., :HALF], "space", backward),
        )

    edges = jnp.concatenate([distribution[:DEPTH], distribution[planes - DEPTH :]], axis=0)
    edge_low, edge_high = both_ways(edges)
    low, high = both_ways(distribution[DEPTH : planes - DEPTH])

    part = pl.pallas_call(
        moments_kernel,
        out_shape=shape(columns, rows, 128),
        in_specs=[SMEM, VMEM],
        out_specs=VMEM,
        compiler_params=PARAMS,
    )(facts, distribution)
    part = part + lax.ppermute(part, "vz", partners)
    total = part + lax.ppermute(part, "vz", opposite)

    outer, inner = pl.pallas_call(
        edges_kernel,
        out_shape=[shape(DEPTH, columns, rows, width)] * 2,
        in_specs=[SMEM, VMEM, VMEM, VMEM],
        out_specs=[VMEM, VMEM],
        scratch_shapes=[pltpu.VMEM((7, rows, width), jnp.float32)],
        compiler_params=PARAMS,
    )(facts, distribution, edge_low, edge_high)
    outer_halo = lax.ppermute(outer, "vz", crossing)
    inner_halo = lax.ppermute(inner, "vz", partners)

    coef, cell = pl.pallas_call(
        coefficients_kernel,
        out_shape=[shape(columns, 5, rows, width), shape(columns, 5, rows, 128)],
        in_specs=[VMEM, VMEM],
        out_specs=[VMEM, VMEM],
        compiler_params=PARAMS,
    )(total, jnp.broadcast_to(collision_rate[:, :, None], (columns, rows, 128)))

    block = (columns, rows, width)
    most, kept = pl.pallas_call(
        main_kernel,
        out_shape=[shape(planes, *block), shape(7, *block)],
        in_specs=[SMEM] + [VMEM] * 8,
        out_specs=[VMEM, VMEM],
        scratch_shapes=[
            pltpu.VMEM((7, rows, width), jnp.float32),
            pltpu.VMEM((planes + DEPTH, *block), jnp.float32),
            pltpu.VMEM((planes + DEPTH, *block), jnp.float32),
            pltpu.VMEM((planes + DEPTH, *block), jnp.float32),
            pltpu.VMEM((planes + DEPTH, *block), jnp.float32),
        ],
        compiler_params=PARAMS,
    )(facts, distribution, low, high, outer, inner, inner_halo, coef, cell)

    def whole(*dims):
        return pl.BlockSpec(dims, lambda i, facts: (0,) * len(dims))

    return pl.pallas_call(
        last_kernel,
        out_shape=shape(planes, *block),
        grid_spec=pltpu.PrefetchScalarGridSpec(
            num_scalar_prefetch=1,
            grid=(1,),
            in_specs=[
                whole(DEPTH, *block),
                whole(DEPTH, *block),
                whole(7, *block),
                whole(columns, 5, rows, width),
                whole(columns, 5, rows, 128),
                pl.BlockSpec(memory_space=pl.ANY),
            ],
            out_specs=pl.BlockSpec(
                (DEPTH, *block),
                lambda i, facts: (lax.rem(facts[0], 2) * (planes // DEPTH - 1), 0, 0, 0),
            ),
            scratch_shapes=[pltpu.VMEM((8, *block), jnp.float32)] * 4,
        ),
        input_output_aliases={6: 0},
        compiler_params=PARAMS,
    )(facts, outer_halo, outer, kept, coef, cell, most)


def solution(mesh):
    return jax.shard_map(
        shards,
        mesh=mesh,
        in_specs=(P("vz", "space", None, None), P("space", None)),
        out_specs=P("vz", "space", None, None),
        check_vma=False,
    )
```

```python
import functools
import math

import jax
import jax.numpy as jnp
from jax import lax
from jax.experimental import pallas as pl
from jax.experimental.pallas import tpu as pltpu
from jax.sharding import PartitionSpec as P

V = 48
WIDTH = V * V
HALF = WIDTH // 2
DEPTH = 3

vel_max = 4.5
step_ratio = 0.1
collision_scale = 0.004
relax_scale = 0.5
spacing = 2.0 * vel_max / V

VMEM_LIMIT = 40 * 1024 * 1024


def speed_of(position):
    return vel_max * (2.0 * position - (V - 1.0)) / V


def lane_grid(first, width, rows=8):
    lane = lax.broadcasted_iota(jnp.int32, (rows, width), 1).astype(jnp.float32) + float(first)
    column = jnp.floor((lane + 0.5) * (1.0 / V))
    return column, lane - V * column


def wide(tile):
    return jnp.concatenate([tile] * (WIDTH // 128), axis=1)


def moments_kernel(slab_ref, f_ref, out_ref, up_ref, down_ref):
    planes, columns = f_ref.shape[0], f_ref.shape[1]
    slab = slab_ref[0]
    chunk = 768
    lane = lax.broadcasted_iota(jnp.int32, (8, 128), 1)
    for column in range(columns):
        totals = [jnp.zeros((8, 1), jnp.float32)] * 5
        for first in range(0, WIDTH, chunk):
            mass = jnp.zeros((8, chunk), jnp.float32)
            flow = jnp.zeros((8, chunk), jnp.float32)
            heat = jnp.zeros((8, chunk), jnp.float32)
            for plane in range(planes):
                cz = speed_of((slab * planes + plane).astype(jnp.float32))
                f = f_ref[plane, column, :, first : first + chunk]
                scaled = f * cz
                mass += f
                flow += scaled
                heat += scaled * cz
            vx, vy = lane_grid(first, chunk)
            cx, cy = speed_of(vx), speed_of(vy)
            parts = (mass, mass * cx, mass * cy, flow, mass * (cx * cx + cy * cy) + heat)
            totals = [t + jnp.sum(p, axis=1, keepdims=True) for t, p in zip(totals, parts)]
        row = jnp.zeros((8, 128), jnp.float32)
        for k in range(5):
            row = jnp.where(lane == k, totals[k], row)
        out_ref[column] = row
    for k in range(planes - 2 * DEPTH):
        up_ref[k] = f_ref[DEPTH + k, :, :, HALF:]
        down_ref[k] = f_ref[DEPTH + k, :, :, :HALF]


def coefficients_kernel(total_ref, rate_ref, coef_ref, cell_ref):
    for column in range(total_ref.shape[0]):
        m0, m1, m2, m3, m4 = (
            jnp.broadcast_to(total_ref[column, :, k : k + 1], (8, 128)) for k in range(5)
        )
        rate = rate_ref[column]
        density = m0 * spacing**3
        ux, uy, uz = m1 / m0, m2 / m0, m3 / m0
        temperature = (m4 / m0 - ux * ux - uy * uy - uz * uz) / 3.0
        stiff = temperature / (spacing * spacing)
        collide, relax = collision_scale * rate, relax_scale * rate
        inverse = 1.0 / (1.0 + relax + 6.0 * collide * stiff)
        middle = collide * inverse * (stiff + 0.5)
        slope = collide * inverse * (0.5 / spacing)
        root = 1.0 / jnp.sqrt(2.0 * math.pi * temperature)
        scale = density * (root * root * root) * (relax * inverse)
        for k, value in enumerate((middle, slope, uz, temperature, inverse)):
            cell_ref[column, k] = value
        vx, vy = lane_grid(0, WIDTH)
        dx, dy = speed_of(vx) - wide(ux), speed_of(vy) - wide(uy)
        middle, slope = wide(middle), wide(slope)
        coef_ref[column, 0] = jnp.where(vx < V - 1.5, middle + slope * dx, 0.0)
        coef_ref[column, 1] = jnp.where(vx > 0.5, middle - slope * dx, 0.0)
        coef_ref[column, 2] = jnp.where(vy < V - 1.5, middle + slope * dy, 0.0)
        coef_ref[column, 3] = jnp.where(vy > 0.5, middle - slope * dy, 0.0)
        coef_ref[column, 4] = wide(scale) * jnp.exp(
            -(dx * dx + dy * dy) / (2.0 * wide(temperature))
        )


def upwind_weights(speed):
    a = step_ratio * jnp.abs(speed)
    return 1.0 - 1.5 * a + 0.5 * a * a, 2.0 * a - a * a, 0.5 * a * a - 0.5 * a


def fill_weights(weight_ref):
    vx, vy = lane_grid(0, WIDTH)
    for k, value in enumerate(upwind_weights(speed_of(vx)) + upwind_weights(speed_of(vy))):
        weight_ref[k] = value
    weight_ref[6] = jnp.where(vy > V // 2 - 0.5, 1.0, 0.0)


def transport_plane(f_ref, plane, low_ref, high_ref, entry, weight_ref, store):
    for column in range(2):
        for part in range(2):
            lanes = pl.ds(part * HALF, HALF)
            f = f_ref[plane, column, :, lanes]
            if part == 1:
                near = low_ref[entry, 1] if column == 0 else f_ref[plane, 0, :, lanes]
                far = low_ref[entry, column]
            else:
                near = f_ref[plane, 1, :, lanes] if column == 0 else high_ref[entry, 0]
                far = high_ref[entry, column]
            swept = (
                weight_ref[0, :, lanes] * f
                + weight_ref[1, :, lanes] * near
                + weight_ref[2, :, lanes] * far
            )
            positive = weight_ref[6, :, lanes] > 0.5
            near = jnp.where(positive, pltpu.roll(swept, 1, 0), pltpu.roll(swept, 7, 0))
            far = jnp.where(positive, pltpu.roll(swept, 2, 0), pltpu.roll(swept, 6, 0))
            store(
                column,
                lanes,
                weight_ref[3, :, lanes] * swept
                + weight_ref[4, :, lanes] * near
                + weight_ref[5, :, lanes] * far,
            )


def edges_kernel(slab_ref, f_ref, low_ref, high_ref, outer_ref, inner_ref, weight_ref):
    planes = f_ref.shape[0]
    odd = lax.rem(slab_ref[0], 2)
    fill_weights(weight_ref)
    for side, target in ((0, outer_ref), (1, inner_ref)):

        def step(k, carry, side=side, target=target):
            place = k + side * DEPTH
            entry = jnp.where(odd == 1, 2 * DEPTH - 1 - place, place)
            plane = jnp.where(entry < DEPTH, entry, entry + planes - 2 * DEPTH)

            def store(column, lanes, value):
                target[k, column, :, lanes] = value

            transport_plane(f_ref, plane, low_ref, high_ref, entry, weight_ref, store)
            return carry

        lax.fori_loop(0, DEPTH, step, 0)


CHUNK = 9


def neighbours(tiles):
    lane = lax.broadcasted_iota(jnp.int32, (8, 128), 1)
    found = []
    for distance in (V, 1):
        ahead = [pltpu.roll(t, 128 - distance, 1) for t in tiles[1:]]
        behind = [pltpu.roll(t, distance, 1) for t in tiles[:-1]]
        inner, outer = lane < 128 - distance, lane >= distance
        found.append([jnp.where(inner, ahead[k], ahead[k + 1]) for k in range(CHUNK)])
        found.append([jnp.where(outer, behind[k + 1], behind[k]) for k in range(CHUNK)])
    return found


class Cell:
    def __init__(self, cell_ref, column, slab, planes):
        odd = lax.rem(slab, 2)
        self.middle, self.slope, self.uz, self.temperature, self.inverse = (
            cell_ref[column, k] for k in range(5)
        )
        self.sign = jnp.where(odd == 1, -1.0, 1.0)
        self.zero = speed_of((slab * planes + odd * (planes - 1)).astype(jnp.float32))

    def distance(self, place):
        return self.zero + self.sign * (place * spacing) - self.uz

    def weights(self, place):
        tilt = self.sign * self.slope * self.distance(place)
        return self.middle + tilt, self.middle - tilt

    def fall(self, place):
        distance = self.distance(place)
        return jnp.exp(-(distance * distance) / (2.0 * self.temperature))


def sweep(places, old, new, source, coef_ref, cell_ref, slab, planes, make=False, also=None):
    per_row = WIDTH // (128 * CHUNK)

    def at(pair, column, first):
        if pair is None:
            return None
        ref, index = pair
        return ref[index, column, :, pl.ds(first, 128)]

    def step(item, carry):
        column = item // per_row
        base = (item - column * per_row) * (128 * CHUNK)
        firsts = [pl.multiple_of(base + 128 * k, 128) for k in range(CHUNK)]
        left = pl.multiple_of(jnp.maximum(base - 128, 0), 128)
        right = pl.multiple_of(jnp.minimum(base + 128 * CHUNK, WIDTH - 128), 128)
        count = 5 if make else 4
        coef = [[coef_ref[column, k, :, pl.ds(f, 128)] for f in firsts] for k in range(count)]
        cell = Cell(cell_ref, column, slab, planes)
        before = [at(old(places[0] - 1), column, f) for f in firsts]
        here = [at(old(places[0]), column, f) for f in firsts]
        for place in places:
            after = [at(old(place + 1), column, f) for f in firsts]
            ends = [at(old(place), column, f) for f in (left, right)]
            shifted = neighbours([ends[0], *here, ends[1]])
            plus, minus = cell.weights(place)
            if make:
                fall = cell.fall(place)
            targets = [new(place)]
            if also is not None and also(place) is not None:
                targets.append(also(place))
            for k, f in enumerate(firsts):
                if make:
                    total = cell.inverse * here[k] + fall * coef[4][k]
                    ref, index = source(place)
                    ref[index, column, :, pl.ds(f, 128)] = total
                else:
                    total = at(source(place), column, f)
                side = plus * after[k]
                if before[k] is not None:
                    side += minus * before[k]
                across = coef[0][k] * shifted[0][k] + coef[1][k] * shifted[1][k]
                along = coef[2][k] * shifted[2][k] + coef[3][k] * shifted[3][k]
                total = (total + side) + (across + along)
                for ref, index in targets:
                    ref[index, column, :, pl.ds(f, 128)] = total
            before, here = here, after
        return carry

    lax.fori_loop(0, 2 * per_row, step, 0)


def main_kernel(
    slab_ref, f_ref, low_ref, high_ref, outer_ref, inner_ref, halo_ref, coef_ref, cell_ref,
    out_ref, kept_ref, weight_ref, zero_ref, source_ref, one_ref, two_ref, new_ref, sem,
):
    planes = f_ref.shape[0]
    slab = slab_ref[0]
    odd = lax.rem(slab, 2)
    fill_weights(weight_ref)

    def transport_step(k, carry):
        plane = jnp.where(odd == 1, planes - 1 - DEPTH - k, DEPTH + k)

        def store(column, lanes, value):
            zero_ref[k, column, :, lanes] = value

        transport_plane(f_ref, plane, low_ref, high_ref, plane - DEPTH, weight_ref, store)
        return carry

    lax.fori_loop(0, planes - 2 * DEPTH, transport_step, 0)

    def start_of(place):
        if place < 0:
            return None
        if place < DEPTH:
            return outer_ref, place
        if place < planes - DEPTH:
            return zero_ref, place - DEPTH
        if place < planes:
            return inner_ref, place - planes + DEPTH
        return halo_ref, planes + DEPTH - 1 - place

    def one(place):
        return None if place < 0 else (one_ref, place)

    def two(place):
        return None if place < 0 else (two_ref, place)

    def source(place):
        return source_ref, place

    def last(place):
        if place < DEPTH:
            return kept_ref, place + 1
        return new_ref, jnp.where(odd == 1, planes - 1 - place, place - DEPTH)

    def first(place):
        return (kept_ref, 0) if place == 0 else None

    rest = (coef_ref, cell_ref, slab, planes)
    sweep(range(0, planes + 2), start_of, one, source, *rest, make=True, also=first)
    sweep(range(0, planes + 1), one, two, source, *rest)
    sweep(range(0, planes), two, last, source, *rest)
    done = pltpu.make_async_copy(
        new_ref, out_ref.at[pl.ds((1 - odd) * DEPTH, planes - DEPTH)], sem
    )
    done.start()
    done.wait()


def last_kernel(
    slab_ref, halo_ref, outer_ref, kept_ref, coef_ref, cell_ref, before_ref,
    out_ref, new_ref, mix_ref, rest_ref, sem,
):
    planes = out_ref.shape[0]
    slab = slab_ref[0]
    odd = lax.rem(slab, 2)
    inside = jnp.where((slab == 0) | (slab == slab_ref[1] - 1), 0.0, 1.0)
    per_row = WIDTH // (128 * CHUNK)

    def spot(place):
        return jnp.where(odd == 1, DEPTH - 1 - place, place)

    def within(read, coef_ref, column, base, firsts):
        left = pl.multiple_of(jnp.maximum(base - 128, 0), 128)
        right = pl.multiple_of(jnp.minimum(base + 128 * CHUNK, WIDTH - 128), 128)
        tiles = [read(f) for f in (left, *firsts, right)]
        shifted = neighbours(tiles)
        results = []
        for k, f in enumerate(firsts):
            coef = [coef_ref[column, c, :, pl.ds(f, 128)] for c in range(4)]
            results.append(
                (coef[0] * shifted[0][k] + coef[1] * shifted[1][k])
                + (coef[2] * shifted[2][k] + coef[3] * shifted[3][k])
            )
        return results

    def walk(body):
        def step(item, carry):
            column = item // per_row
            base = (item - column * per_row) * (128 * CHUNK)
            firsts = [pl.multiple_of(base + 128 * k, 128) for k in range(CHUNK)]
            cell = Cell(cell_ref, column, slab, planes)
            body(column, base, firsts, cell)
            return carry

        lax.fori_loop(0, 2 * per_row, step, 0)

    def first(column, base, firsts, cell):
        plus1, minus1 = cell.weights(-1)
        plus2, minus2 = cell.weights(-2)
        next0, into0 = cell.weights(0)
        _, into1 = cell.weights(1)
        _, into2 = cell.weights(2)
        into0 = into0 * inside
        fall1, fall2 = cell.fall(-1), cell.fall(-2)
        flat = within(lambda f: halo_ref[0, column, :, pl.ds(f, 128)], coef_ref, column, base, firsts)
        for k, f in enumerate(firsts):
            lanes = pl.ds(f, 128)
            h1, h2, h3 = (halo_ref[i, column, :, lanes] for i in range(3))
            bell = coef_ref[column, 4, :, lanes]
            source1 = cell.inverse * h1 + fall1 * bell
            source2 = cell.inverse * h2 + fall2 * bell
            swept = minus1 * h2 + flat[k]
            once = source1 + plus1 * outer_ref[0, column, :, lanes] + swept
            mix_ref[column, :, lanes] = swept + 2.0 * once
            own = kept_ref[0, column, :, lanes] + into0 * h1
            other = source2 + plus2 * h1 + minus2 * h3
            rest_ref[column, :, lanes] = (
                kept_ref[1, column, :, lanes]
                + (next0 * into1 * into0) * h1
                + into0 * (source1 + plus1 * own + minus1 * other)
            )
            new_ref[spot(1), column, :, lanes] = kept_ref[2, column, :, lanes] + (into1 * into0) * (
                once + 2.0 * flat[k]
            )
            new_ref[spot(2), column, :, lanes] = (
                kept_ref[3, column, :, lanes] + (into2 * into1 * into0) * h1
            )

    def second(column, base, firsts, cell):
        into0 = cell.weights(0)[1] * inside
        flat = within(lambda f: mix_ref[column, :, pl.ds(f, 128)], coef_ref, column, base, firsts)
        for k, f in enumerate(firsts):
            lanes = pl.ds(f, 128)
            new_ref[spot(0), column, :, lanes] = rest_ref[column, :, lanes] + into0 * flat[k]

    walk(first)
    walk(second)
    done = pltpu.make_async_copy(
        new_ref, out_ref.at[pl.ds(odd * (planes - DEPTH), DEPTH)], sem
    )
    done.start()
    done.wait()


def shape(*dims):
    return jax.ShapeDtypeStruct(dims, jnp.float32)


PARAMS = pltpu.CompilerParams(vmem_limit_bytes=VMEM_LIMIT)
HEAVY = pl.CostEstimate(flops=20_000_000_000, bytes_accessed=20_000_000, transcendentals=0)
SMEM = pl.BlockSpec(memory_space=pltpu.SMEM)
VMEM = pl.BlockSpec(memory_space=pltpu.VMEM)
ANY = pl.BlockSpec(memory_space=pl.ANY)


def shards(distribution, collision_rate):
    planes, columns, rows, width = distribution.shape
    spaces, slabs = lax.axis_size("space"), lax.axis_size("vz")
    slab = lax.axis_index("vz").astype(jnp.int32)
    facts = jnp.stack([slab, jnp.int32(slabs)])

    forward = [(i, (i + 1) % spaces) for i in range(spaces)]
    backward = [(b, a) for a, b in forward]
    partners = [(i, i ^ 1) for i in range(slabs)]
    crossing = [(i, i + 1) for i in range(1, slabs - 1, 2)]
    crossing += [(b, a) for a, b in crossing]
    opposite = [(i, slabs - 1 - i) for i in range(slabs)]

    def both_ways(up, down):
        return lax.ppermute(up, "space", forward), lax.ppermute(down, "space", backward)

    groups = distribution.reshape(planes // DEPTH, DEPTH, columns, rows, width)
    groups = groups[:: planes // DEPTH - 1]
    ends = (2 * DEPTH, columns, rows, HALF)
    up, down, later = lax.optimization_barrier(
        (groups[..., HALF:].reshape(ends), groups[..., :HALF].reshape(ends), distribution)
    )
    edge_low, edge_high = both_ways(up, down)

    half = (planes - 2 * DEPTH, columns, rows, HALF)
    part, up, down = pl.pallas_call(
        moments_kernel,
        out_shape=[shape(columns, rows, 128), shape(*half), shape(*half)],
        in_specs=[SMEM, VMEM],
        out_specs=[VMEM] * 3,
        compiler_params=PARAMS,
    )(facts, later)
    low, high = both_ways(up, down)
    part = part + lax.ppermute(part, "vz", partners)
    edge_low, edge_high, _ = lax.optimization_barrier((edge_low, edge_high, part))
    total = part + lax.ppermute(part, "vz", opposite)

    outer, inner = pl.pallas_call(
        edges_kernel,
        out_shape=[shape(DEPTH, columns, rows, width)] * 2,
        in_specs=[SMEM, VMEM, VMEM, VMEM],
        out_specs=[VMEM, VMEM],
        scratch_shapes=[pltpu.VMEM((7, rows, width), jnp.float32)],
        compiler_params=PARAMS,
        cost_estimate=HEAVY,
    )(facts, distribution, edge_low, edge_high)
    outer_halo = lax.ppermute(outer, "vz", crossing)
    inner_halo = lax.ppermute(inner, "vz", partners)

    coef, cell = pl.pallas_call(
        coefficients_kernel,
        out_shape=[shape(columns, 5, rows, width), shape(columns, 5, rows, 128)],
        in_specs=[VMEM, VMEM],
        out_specs=[VMEM, VMEM],
        compiler_params=PARAMS,
        cost_estimate=HEAVY,
    )(total, jnp.broadcast_to(collision_rate[:, :, None], (columns, rows, 128)))

    block = (columns, rows, width)
    most, kept = pl.pallas_call(
        main_kernel,
        out_shape=[shape(planes, *block), shape(4, *block)],
        in_specs=[SMEM] + [VMEM] * 8,
        out_specs=[ANY, VMEM],
        scratch_shapes=[
            pltpu.VMEM((7, rows, width), jnp.float32),
            pltpu.VMEM((planes - 2 * DEPTH, *block), jnp.float32),
            pltpu.VMEM((planes + 2, *block), jnp.float32),
            pltpu.VMEM((planes + 2, *block), jnp.float32),
            pltpu.VMEM((planes + 1, *block), jnp.float32),
            pltpu.VMEM((planes - DEPTH, *block), jnp.float32),
            pltpu.SemaphoreType.DMA,
        ],
        compiler_params=PARAMS,
        cost_estimate=HEAVY,
    )(facts, distribution, low, high, outer, inner, inner_halo, coef, cell)

    return pl.pallas_call(
        last_kernel,
        out_shape=shape(planes, *block),
        in_specs=[SMEM] + [VMEM] * 5 + [ANY],
        out_specs=ANY,
        scratch_shapes=[
            pltpu.VMEM((DEPTH, *block), jnp.float32),
            pltpu.VMEM(block, jnp.float32),
            pltpu.VMEM(block, jnp.float32),
            pltpu.SemaphoreType.DMA,
        ],
        input_output_aliases={6: 0},
        compiler_params=PARAMS,
    )(facts, outer_halo, outer, kept, coef, cell, most)


def solution(mesh):
    return jax.shard_map(
        shards,
        mesh=mesh,
        in_specs=(P("vz", "space", None, None), P("space", None)),
        out_specs=P("vz", "space", None, None),
        check_vma=False,
    )
```

```python
import functools
import math

import jax
import jax.numpy as jnp
from jax import lax
from jax.experimental import pallas as pl
from jax.experimental.pallas import tpu as pltpu
from jax.sharding import PartitionSpec as P

V = 48
WIDTH = V * V
HALF = WIDTH // 2
DEPTH = 3

vel_max = 4.5
step_ratio = 0.1
collision_scale = 0.004
relax_scale = 0.5
spacing = 2.0 * vel_max / V

VMEM_LIMIT = 40 * 1024 * 1024


def speed_of(position):
    return vel_max * (2.0 * position - (V - 1.0)) / V


def lane_grid(first, width, rows=8):
    lane = lax.broadcasted_iota(jnp.int32, (rows, width), 1).astype(jnp.float32) + float(first)
    column = jnp.floor((lane + 0.5) * (1.0 / V))
    return column, lane - V * column


def wide(tile):
    return jnp.concatenate([tile] * (WIDTH // 128), axis=1)


def moments_kernel(slab_ref, f_ref, out_ref, up_ref, down_ref):
    planes, columns = f_ref.shape[0], f_ref.shape[1]
    slab = slab_ref[0]
    chunk = 768
    lane = lax.broadcasted_iota(jnp.int32, (8, 128), 1)
    for column in range(columns):
        totals = [jnp.zeros((8, 1), jnp.float32)] * 5
        for first in range(0, WIDTH, chunk):
            mass = jnp.zeros((8, chunk), jnp.float32)
            flow = jnp.zeros((8, chunk), jnp.float32)
            heat = jnp.zeros((8, chunk), jnp.float32)
            for plane in range(planes):
                cz = speed_of((slab * planes + plane).astype(jnp.float32))
                f = f_ref[plane, column, :, first : first + chunk]
                scaled = f * cz
                mass += f
                flow += scaled
                heat += scaled * cz
            vx, vy = lane_grid(first, chunk)
            cx, cy = speed_of(vx), speed_of(vy)
            parts = (mass, mass * cx, mass * cy, flow, mass * (cx * cx + cy * cy) + heat)
            totals = [t + jnp.sum(p, axis=1, keepdims=True) for t, p in zip(totals, parts)]
        row = jnp.zeros((8, 128), jnp.float32)
        for k in range(5):
            row = jnp.where(lane == k, totals[k], row)
        out_ref[column] = row
    for k in range(planes - 2 * DEPTH):
        up_ref[k] = f_ref[DEPTH + k, :, :, HALF:]
        down_ref[k] = f_ref[DEPTH + k, :, :, :HALF]


def coefficients_kernel(total_ref, rate_ref, coef_ref, cell_ref):
    for column in range(total_ref.shape[0]):
        m0, m1, m2, m3, m4 = (
            jnp.broadcast_to(total_ref[column, :, k : k + 1], (8, 128)) for k in range(5)
        )
        rate = rate_ref[column]
        density = m0 * spacing**3
        ux, uy, uz = m1 / m0, m2 / m0, m3 / m0
        temperature = (m4 / m0 - ux * ux - uy * uy - uz * uz) / 3.0
        stiff = temperature / (spacing * spacing)
        collide, relax = collision_scale * rate, relax_scale * rate
        inverse = 1.0 / (1.0 + relax + 6.0 * collide * stiff)
        middle = collide * inverse * (stiff + 0.5)
        slope = collide * inverse * (0.5 / spacing)
        root = 1.0 / jnp.sqrt(2.0 * math.pi * temperature)
        scale = density * (root * root * root) * (relax * inverse)
        for k, value in enumerate((middle, slope, uz, temperature, inverse)):
            cell_ref[column, k] = value
        vx, vy = lane_grid(0, WIDTH)
        dx, dy = speed_of(vx) - wide(ux), speed_of(vy) - wide(uy)
        middle, slope = wide(middle), wide(slope)
        coef_ref[column, 0] = jnp.where(vx < V - 1.5, middle + slope * dx, 0.0)
        coef_ref[column, 1] = jnp.where(vx > 0.5, middle - slope * dx, 0.0)
        coef_ref[column, 2] = jnp.where(vy < V - 1.5, middle + slope * dy, 0.0)
        coef_ref[column, 3] = jnp.where(vy > 0.5, middle - slope * dy, 0.0)
        coef_ref[column, 4] = wide(scale) * jnp.exp(
            -(dx * dx + dy * dy) / (2.0 * wide(temperature))
        )


def upwind_weights(speed):
    a = step_ratio * jnp.abs(speed)
    return 1.0 - 1.5 * a + 0.5 * a * a, 2.0 * a - a * a, 0.5 * a * a - 0.5 * a


def fill_weights(weight_ref):
    vx, vy = lane_grid(0, WIDTH)
    for k, value in enumerate(upwind_weights(speed_of(vx)) + upwind_weights(speed_of(vy))):
        weight_ref[k] = value
    weight_ref[6] = jnp.where(vy > V // 2 - 0.5, 1.0, 0.0)


def transport_plane(f_ref, plane, low_ref, high_ref, entry, weight_ref, store):
    for column in range(2):
        for part in range(2):
            lanes = pl.ds(part * HALF, HALF)
            f = f_ref[plane, column, :, lanes]
            if part == 1:
                near = low_ref[entry, 1] if column == 0 else f_ref[plane, 0, :, lanes]
                far = low_ref[entry, column]
            else:
                near = f_ref[plane, 1, :, lanes] if column == 0 else high_ref[entry, 0]
                far = high_ref[entry, column]
            swept = (
                weight_ref[0, :, lanes] * f
                + weight_ref[1, :, lanes] * near
                + weight_ref[2, :, lanes] * far
            )
            positive = weight_ref[6, :, lanes] > 0.5
            near = jnp.where(positive, pltpu.roll(swept, 1, 0), pltpu.roll(swept, 7, 0))
            far = jnp.where(positive, pltpu.roll(swept, 2, 0), pltpu.roll(swept, 6, 0))
            store(
                column,
                lanes,
                weight_ref[3, :, lanes] * swept
                + weight_ref[4, :, lanes] * near
                + weight_ref[5, :, lanes] * far,
            )


def edges_kernel(slab_ref, f_ref, low_ref, high_ref, outer_ref, inner_ref, weight_ref):
    planes = f_ref.shape[0]
    odd = lax.rem(slab_ref[0], 2)
    fill_weights(weight_ref)
    for side, target in ((0, outer_ref), (1, inner_ref)):

        def step(k, carry, side=side, target=target):
            place = k + side * DEPTH
            entry = jnp.where(odd == 1, 2 * DEPTH - 1 - place, place)
            plane = jnp.where(entry < DEPTH, entry, entry + planes - 2 * DEPTH)

            def store(column, lanes, value):
                target[k, column, :, lanes] = value

            transport_plane(f_ref, plane, low_ref, high_ref, entry, weight_ref, store)
            return carry

        lax.fori_loop(0, DEPTH, step, 0)


CHUNK = 9


def neighbours(tiles):
    lane = lax.broadcasted_iota(jnp.int32, (8, 128), 1)
    found = []
    for distance in (V, 1):
        ahead = [pltpu.roll(t, 128 - distance, 1) for t in tiles[1:]]
        behind = [pltpu.roll(t, distance, 1) for t in tiles[:-1]]
        inner, outer = lane < 128 - distance, lane >= distance
        found.append([jnp.where(inner, ahead[k], ahead[k + 1]) for k in range(CHUNK)])
        found.append([jnp.where(outer, behind[k + 1], behind[k]) for k in range(CHUNK)])
    return found


class Cell:
    def __init__(self, cell_ref, column, slab, planes):
        odd = lax.rem(slab, 2)
        self.middle, self.slope, self.uz, self.temperature, self.inverse = (
            cell_ref[column, k] for k in range(5)
        )
        self.sign = jnp.where(odd == 1, -1.0, 1.0)
        self.zero = speed_of((slab * planes + odd * (planes - 1)).astype(jnp.float32))

    def distance(self, place):
        return self.zero + self.sign * (place * spacing) - self.uz

    def weights(self, place):
        tilt = self.sign * self.slope * self.distance(place)
        return self.middle + tilt, self.middle - tilt

    def fall(self, place):
        distance = self.distance(place)
        return jnp.exp(-(distance * distance) / (2.0 * self.temperature))


def sweep(places, old, new, source, coef_ref, cell_ref, slab, planes, make=False, also=None):
    per_row = WIDTH // (128 * CHUNK)

    def at(pair, column, first):
        if pair is None:
            return None
        ref, index = pair
        return ref[index, column, :, pl.ds(first, 128)]

    def step(item, carry):
        column = item // per_row
        base = (item - column * per_row) * (128 * CHUNK)
        firsts = [pl.multiple_of(base + 128 * k, 128) for k in range(CHUNK)]
        left = pl.multiple_of(jnp.maximum(base - 128, 0), 128)
        right = pl.multiple_of(jnp.minimum(base + 128 * CHUNK, WIDTH - 128), 128)
        count = 5 if make else 4
        coef = [[coef_ref[column, k, :, pl.ds(f, 128)] for f in firsts] for k in range(count)]
        cell = Cell(cell_ref, column, slab, planes)
        before = [at(old(places[0] - 1), column, f) for f in firsts]
        here = [at(old(places[0]), column, f) for f in firsts]
        for place in places:
            after = [at(old(place + 1), column, f) for f in firsts]
            ends = [at(old(place), column, f) for f in (left, right)]
            shifted = neighbours([ends[0], *here, ends[1]])
            plus, minus = cell.weights(place)
            if make:
                fall = cell.fall(place)
            targets = [new(place)]
            if also is not None and also(place) is not None:
                targets.append(also(place))
            for k, f in enumerate(firsts):
                if make:
                    total = cell.inverse * here[k] + fall * coef[4][k]
                    ref, index = source(place)
                    ref[index, column, :, pl.ds(f, 128)] = total
                else:
                    total = at(source(place), column, f)
                side = plus * after[k]
                if before[k] is not None:
                    side += minus * before[k]
                across = coef[0][k] * shifted[0][k] + coef[1][k] * shifted[1][k]
                along = coef[2][k] * shifted[2][k] + coef[3][k] * shifted[3][k]
                total = (total + side) + (across + along)
                for ref, index in targets:
                    ref[index, column, :, pl.ds(f, 128)] = total
            before, here = here, after
        return carry

    lax.fori_loop(0, 2 * per_row, step, 0)


def main_kernel(
    slab_ref, f_ref, low_ref, high_ref, outer_ref, inner_ref, halo_ref, coef_ref, cell_ref,
    out_ref, kept_ref, weight_ref, zero_ref, source_ref, one_ref, two_ref, new_ref, sem,
):
    planes = f_ref.shape[0]
    slab = slab_ref[0]
    odd = lax.rem(slab, 2)
    fill_weights(weight_ref)

    def transport_step(k, carry):
        plane = jnp.where(odd == 1, planes - 1 - DEPTH - k, DEPTH + k)

        def store(column, lanes, value):
            zero_ref[k, column, :, lanes] = value

        transport_plane(f_ref, plane, low_ref, high_ref, plane - DEPTH, weight_ref, store)
        return carry

    lax.fori_loop(0, planes - 2 * DEPTH, transport_step, 0)

    def start_of(place):
        if place < 0:
            return None
        if place < DEPTH:
            return outer_ref, place
        if place < planes - DEPTH:
            return zero_ref, place - DEPTH
        if place < planes:
            return inner_ref, place - planes + DEPTH
        return halo_ref, planes + DEPTH - 1 - place

    def one(place):
        return None if place < 0 else (one_ref, place)

    def two(place):
        return None if place < 0 else (two_ref, place)

    def source(place):
        return source_ref, place

    def last(place):
        if place < DEPTH:
            return kept_ref, place + 1
        return new_ref, jnp.where(odd == 1, planes - 1 - place, place - DEPTH)

    def first(place):
        return (kept_ref, 0) if place == 0 else None

    rest = (coef_ref, cell_ref, slab, planes)
    sweep(range(0, planes + 2), start_of, one, source, *rest, make=True, also=first)
    sweep(range(0, planes + 1), one, two, source, *rest)
    sweep(range(0, planes), two, last, source, *rest)
    done = pltpu.make_async_copy(
        new_ref, out_ref.at[pl.ds((1 - odd) * DEPTH, planes - DEPTH)], sem
    )
    done.start()
    done.wait()


def last_kernel(
    slab_ref, halo_ref, outer_ref, kept_ref, coef_ref, cell_ref, before_ref,
    out_ref, new_ref, mix_ref, rest_ref, sem,
):
    planes = out_ref.shape[0]
    slab = slab_ref[0]
    odd = lax.rem(slab, 2)
    inside = jnp.where((slab == 0) | (slab == slab_ref[1] - 1), 0.0, 1.0)
    per_row = WIDTH // (128 * CHUNK)

    def spot(place):
        return jnp.where(odd == 1, DEPTH - 1 - place, place)

    def within(read, coef_ref, column, base, firsts):
        left = pl.multiple_of(jnp.maximum(base - 128, 0), 128)
        right = pl.multiple_of(jnp.minimum(base + 128 * CHUNK, WIDTH - 128), 128)
        tiles = [read(f) for f in (left, *firsts, right)]
        shifted = neighbours(tiles)
        results = []
        for k, f in enumerate(firsts):
            coef = [coef_ref[column, c, :, pl.ds(f, 128)] for c in range(4)]
            results.append(
                (coef[0] * shifted[0][k] + coef[1] * shifted[1][k])
                + (coef[2] * shifted[2][k] + coef[3] * shifted[3][k])
            )
        return results

    def walk(body):
        def step(item, carry):
            column = item // per_row
            base = (item - column * per_row) * (128 * CHUNK)
            firsts = [pl.multiple_of(base + 128 * k, 128) for k in range(CHUNK)]
            cell = Cell(cell_ref, column, slab, planes)
            body(column, base, firsts, cell)
            return carry

        lax.fori_loop(0, 2 * per_row, step, 0)

    def first(column, base, firsts, cell):
        plus1, minus1 = cell.weights(-1)
        plus2, minus2 = cell.weights(-2)
        next0, into0 = cell.weights(0)
        _, into1 = cell.weights(1)
        _, into2 = cell.weights(2)
        into0 = into0 * inside
        fall1, fall2 = cell.fall(-1), cell.fall(-2)
        flat = within(lambda f: halo_ref[0, column, :, pl.ds(f, 128)], coef_ref, column, base, firsts)
        for k, f in enumerate(firsts):
            lanes = pl.ds(f, 128)
            h1, h2, h3 = (halo_ref[i, column, :, lanes] for i in range(3))
            bell = coef_ref[column, 4, :, lanes]
            source1 = cell.inverse * h1 + fall1 * bell
            source2 = cell.inverse * h2 + fall2 * bell
            swept = minus1 * h2 + flat[k]
            once = source1 + plus1 * outer_ref[0, column, :, lanes] + swept
            mix_ref[column, :, lanes] = swept + 2.0 * once
            own = kept_ref[0, column, :, lanes] + into0 * h1
            other = source2 + plus2 * h1 + minus2 * h3
            rest_ref[column, :, lanes] = (
                kept_ref[1, column, :, lanes]
                + (next0 * into1 * into0) * h1
                + into0 * (source1 + plus1 * own + minus1 * other)
            )
            new_ref[spot(1), column, :, lanes] = kept_ref[2, column, :, lanes] + (into1 * into0) * (
                once + 2.0 * flat[k]
            )
            new_ref[spot(2), column, :, lanes] = (
                kept_ref[3, column, :, lanes] + (into2 * into1 * into0) * h1
            )

    def second(column, base, firsts, cell):
        into0 = cell.weights(0)[1] * inside
        flat = within(lambda f: mix_ref[column, :, pl.ds(f, 128)], coef_ref, column, base, firsts)
        for k, f in enumerate(firsts):
            lanes = pl.ds(f, 128)
            new_ref[spot(0), column, :, lanes] = rest_ref[column, :, lanes] + into0 * flat[k]

    def copy(place, count, sem):
        held = jnp.where(odd == 1, DEPTH - place - count, place)
        return pltpu.make_async_copy(
            new_ref.at[pl.ds(held, count)],
            out_ref.at[pl.ds(held + odd * (planes - DEPTH), count)],
            sem,
        )

    walk(first)
    outer = copy(1, DEPTH - 1, sem.at[1])
    outer.start()
    walk(second)
    nearest = copy(0, 1, sem.at[0])
    nearest.start()
    outer.wait()
    nearest.wait()


def shape(*dims):
    return jax.ShapeDtypeStruct(dims, jnp.float32)


PARAMS = pltpu.CompilerParams(vmem_limit_bytes=VMEM_LIMIT)
HEAVY = pl.CostEstimate(flops=20_000_000_000, bytes_accessed=20_000_000, transcendentals=0)
SMEM = pl.BlockSpec(memory_space=pltpu.SMEM)
VMEM = pl.BlockSpec(memory_space=pltpu.VMEM)
ANY = pl.BlockSpec(memory_space=pl.ANY)


def shards(distribution, collision_rate):
    planes, columns, rows, width = distribution.shape
    spaces, slabs = lax.axis_size("space"), lax.axis_size("vz")
    slab = lax.axis_index("vz").astype(jnp.int32)
    facts = jnp.stack([slab, jnp.int32(slabs)])

    forward = [(i, (i + 1) % spaces) for i in range(spaces)]
    backward = [(b, a) for a, b in forward]
    partners = [(i, i ^ 1) for i in range(slabs)]
    crossing = [(i, i + 1) for i in range(1, slabs - 1, 2)]
    crossing += [(b, a) for a, b in crossing]
    opposite = [(i, slabs - 1 - i) for i in range(slabs)]

    def both_ways(up, down):
        return lax.ppermute(up, "space", forward), lax.ppermute(down, "space", backward)

    groups = distribution.reshape(planes // DEPTH, DEPTH, columns, rows, width)
    groups = groups[:: planes // DEPTH - 1]
    ends = (2 * DEPTH, columns, rows, HALF)
    up, down, later = lax.optimization_barrier(
        (groups[..., HALF:].reshape(ends), groups[..., :HALF].reshape(ends), distribution)
    )
    edge_low, edge_high = both_ways(up, down)

    half = (planes - 2 * DEPTH, columns, rows, HALF)
    part, up, down = pl.pallas_call(
        moments_kernel,
        out_shape=[shape(columns, rows, 128), shape(*half), shape(*half)],
        in_specs=[SMEM, VMEM],
        out_specs=[VMEM] * 3,
        compiler_params=PARAMS,
    )(facts, later)
    low, high = both_ways(up, down)
    part = part + lax.ppermute(part, "vz", partners)
    edge_low, edge_high, _ = lax.optimization_barrier((edge_low, edge_high, part))
    total = part + lax.ppermute(part, "vz", opposite)

    outer, inner = pl.pallas_call(
        edges_kernel,
        out_shape=[shape(DEPTH, columns, rows, width)] * 2,
        in_specs=[SMEM, VMEM, VMEM, VMEM],
        out_specs=[VMEM, VMEM],
        scratch_shapes=[pltpu.VMEM((7, rows, width), jnp.float32)],
        compiler_params=PARAMS,
        cost_estimate=HEAVY,
    )(facts, distribution, edge_low, edge_high)
    outer_halo = lax.ppermute(outer, "vz", crossing)
    inner_halo = lax.ppermute(inner, "vz", partners)

    coef, cell = pl.pallas_call(
        coefficients_kernel,
        out_shape=[shape(columns, 5, rows, width), shape(columns, 5, rows, 128)],
        in_specs=[VMEM, VMEM],
        out_specs=[VMEM, VMEM],
        compiler_params=PARAMS,
        cost_estimate=HEAVY,
    )(total, jnp.broadcast_to(collision_rate[:, :, None], (columns, rows, 128)))

    block = (columns, rows, width)
    most, kept = pl.pallas_call(
        main_kernel,
        out_shape=[shape(planes, *block), shape(4, *block)],
        in_specs=[SMEM] + [VMEM] * 8,
        out_specs=[ANY, VMEM],
        scratch_shapes=[
            pltpu.VMEM((7, rows, width), jnp.float32),
            pltpu.VMEM((planes - 2 * DEPTH, *block), jnp.float32),
            pltpu.VMEM((planes + 2, *block), jnp.float32),
            pltpu.VMEM((planes + 2, *block), jnp.float32),
            pltpu.VMEM((planes + 1, *block), jnp.float32),
            pltpu.VMEM((planes - DEPTH, *block), jnp.float32),
            pltpu.SemaphoreType.DMA,
        ],
        compiler_params=PARAMS,
    )(facts, distribution, low, high, outer, inner, inner_halo, coef, cell)

    return pl.pallas_call(
        last_kernel,
        out_shape=shape(planes, *block),
        in_specs=[SMEM] + [VMEM] * 5 + [ANY],
        out_specs=ANY,
        scratch_shapes=[
            pltpu.VMEM((DEPTH, *block), jnp.float32),
            pltpu.VMEM(block, jnp.float32),
            pltpu.VMEM(block, jnp.float32),
            pltpu.SemaphoreType.DMA((2,)),
        ],
        input_output_aliases={6: 0},
        compiler_params=PARAMS,
    )(facts, outer_halo, outer, kept, coef, cell, most)


def solution(mesh):
    return jax.shard_map(
        shards,
        mesh=mesh,
        in_specs=(P("vz", "space", None, None), P("space", None)),
        out_specs=P("vz", "space", None, None),
        check_vma=False,
    )
```
